32 devices in a mesh: pose: 2 (over y), grid: 8 (over z, x), depth: 2 (over core).
Axes of the slice: x: 2, y: 2, z: 4, core: 2. Of those that a mesh axis runs over, the one named last changes fastest.
Arguments:
- row_block: float32 [2048, 2048], P(('pose', 'grid'), 'depth'), parts along dimension 0, may hold values from -0.125 to 0.125
- column_block: float32 [4096, 12288], P(('pose', 'depth'), 'grid'), parts along dimension 0, may hold values from -6 to 6
- density_slab: float32 [2048, 12288], P(('pose', 'depth'), 'grid'), parts along dimension 0, may hold values from -6 to 6
Outputs:
- purified: float32 [2048, 12288], P(('pose', 'depth'), 'grid'), parts along dimension 0
The draws below stay inside these ranges and needn't reach their ends.
There are 2 independent parts, one for each index of `pose`. The reference program is written for one: setup_inputs(seed, part) draws one part's arguments, and reference() takes and returns one part's arrays. A program takes and returns all parts, laid end to end along the dimension named above; each array names one. Nothing has to cross between parts.
All inputs are finite; a program needn't handle non-finite values.
Results may differ from the reference program's by a relative error of at most 0.00005.
Values sent between devices are 32-bit elements; how exact they have to be, the bound alone decides.
A program may use at most 64 MiB of HBM per device.

```python
import jax
import jax.numpy as jnp
from jax import lax

ROWS = 1024
K = 2048
N = 12288


def block_levels(rng, shape, pieces, least, largest):
    factor_of, own = 1.0, jax.random.fold_in(rng, 6)
    for dim, blocks in pieces:
        draws = jnp.exp(jax.random.uniform(jax.random.fold_in(own, dim), (blocks,), jnp.float32, least / len(pieces), largest / len(pieces)))
        factor_of = factor_of * jnp.repeat(draws, shape[dim] // blocks).reshape([-1 if axis == dim else 1 for axis in range(len(shape))])
    return factor_of


def normal_values(own_key, shape, deviation, most, split=(), held_as=jnp.bfloat16):
    drawn = deviation * jax.random.normal(own_key, shape, jnp.float32)
    if split:
        drawn = drawn * block_levels(own_key, shape, split, -0.22, 0.18)
    return jnp.clip(drawn, -most, most).astype(held_as)


def setup_inputs(seed: int = 0, part: int = 0) -> dict:
    streams_of = jax.random.split(jax.random.key(seed), 4)
    own_keys = jax.random.split(jax.random.fold_in(streams_of[3], part), 4)
    return {
        "row_block": normal_values(own_keys[0], (ROWS, K), K ** -0.5, 0.125, ((0, 8), (1, 2)), jnp.float32),
        "column_block": normal_values(own_keys[1], (K, N), 1.0, 6.0, ((0, 2), (1, 8)), jnp.float32),
        "density_slab": normal_values(own_keys[2], (ROWS, N), 1.0, 6.0, ((0, 2), (1, 8)), jnp.float32),
    }


def reference(row_block, column_block, density_slab):
    squared = jnp.dot(row_block, column_block, preferred_element_type=jnp.float32, precision=lax.Precision.HIGHEST)
    return 2.0 * density_slab - squared
```

```python
import functools

import jax
import jax.numpy as jnp
from jax import lax
from jax.experimental import pallas as pl
from jax.experimental.pallas import tpu as pltpu
from jax.sharding import PartitionSpec as P

MESH = pl.DeviceIdType.MESH
F32, BF16 = jnp.float32, jnp.bfloat16
TILE = 256


def split(value):
    high = value.astype(BF16)
    return high, (value - high.astype(F32)).astype(BF16)


def kernel(
    Z, X, C,
    a_hbm, b_hbm, d_hbm, o_hbm,
    a_all, b_raw, b_high, b_low, a_pair, share, other, slab, result,
    load_sem, b_sem, out_sem, zrecv, xrecv, zsend, xsend, crecv, csend,
):
    grid_at, core = lax.axis_index("grid"), lax.axis_index("depth")
    z, x = grid_at // X, grid_at % X
    G = Z * X
    half = G // 2
    R, K = a_hbm.shape
    N = b_hbm.shape[1]
    piece = R // C
    b_parts = b_sem.shape[0]
    b_rows = K // b_parts

    def rows_of(g):
        return pl.ds(pl.multiple_of(g * R, R), R)

    own_load = pltpu.make_async_copy(a_hbm, a_all.at[rows_of(grid_at)], load_sem.at[0])
    slab_load = pltpu.make_async_copy(d_hbm, slab, load_sem.at[1])
    own_load.start()
    b_loads = []
    for part in range(b_parts):
        rows = pl.ds(part * b_rows, b_rows)
        b_loads.append(pltpu.make_async_copy(b_hbm.at[rows], b_raw.at[rows], b_sem.at[part]))
        b_loads[-1].start()
    slab_load.start()

    barrier = pltpu.get_barrier_semaphore()

    @pl.when(z > 0)
    def _():
        pl.semaphore_signal(barrier, inc=1, device_id={"grid": grid_at - X}, device_id_type=MESH)

    @pl.when(z < Z - 1)
    def _():
        pl.semaphore_signal(barrier, inc=1, device_id={"grid": grid_at + X}, device_id_type=MESH)

    def beside(k):
        return z * X + lax.rem(x + k, X)

    for k in range(1, X):
        pl.semaphore_signal(barrier, inc=1, device_id={"grid": beside(k)}, device_id_type=MESH)
    pl.semaphore_signal(barrier, inc=1, device_id={"depth": 1 - core}, device_id_type=MESH)
    pl.semaphore_wait(barrier, X + (z > 0).astype(jnp.int32) + (z < Z - 1).astype(jnp.int32))

    def piece_rows(g, c):
        return pl.ds(pl.multiple_of(g * R + c * piece, piece), piece)

    def along_z(src, zb, c, step):
        way = 0 if step > 0 else 1
        return pltpu.make_async_remote_copy(
            src, a_all.at[piece_rows(zb * X + x, c)], zsend.at[way, zb], zrecv.at[zb, c],
            device_id={"grid": grid_at + step * X}, device_id_type=MESH)

    def along_x(src, zb, c, k):
        return pltpu.make_async_remote_copy(
            src, a_all.at[piece_rows(zb * X + x, c)], xsend.at[k - 1, zb], xrecv.at[zb * X + x],
            device_id={"grid": beside(k)}, device_id_type=MESH)

    for c in range(C):
        src = a_hbm.at[pl.ds(c * piece, piece)]

        @pl.when(z < Z - 1)
        def _():
            along_z(src, z, c, 1).start()

        @pl.when(z > 0)
        def _():
            along_z(src, z, c, -1).start()

        for k in range(1, X):
            along_x(src, z, c, k).start()

    def relay(d, c, step):
        zb = z - step * d

        @pl.when(jnp.logical_and(zb >= 0, zb < Z))
        def _():
            src = a_all.at[piece_rows(zb * X + x, c)]
            along_z(src, zb, c, step).wait_recv()
            onward = z + step

            @pl.when(jnp.logical_and(onward >= 0, onward < Z))
            def _():
                along_z(src, zb, c, step).start()

            for k in range(1, X):
                along_x(src, zb, c, k).start()

    def exchange(g):
        return pltpu.make_async_remote_copy(
            share.at[rows_of(g)], other.at[rows_of(lax.rem(g, half))],
            csend.at[lax.rem(g, half)], crecv.at[lax.rem(g, half)],
            device_id={"depth": 1 - core}, device_id_type=MESH)

    def compute(g):
        high, low = split(a_all[rows_of(g), :])
        a_pair[0:R, :] = high
        a_pair[R:2 * R, :] = low

        @pl.loop(0, N // TILE)
        def _(t):
            cols = pl.ds(pl.multiple_of(t * TILE, TILE), TILE)
            both = jnp.dot(a_pair[...], b_high[:, cols], preferred_element_type=F32)
            cross = jnp.dot(a_pair[0:R, :], b_low[:, cols], preferred_element_type=F32)
            share[rows_of(g), cols] = both[0:R] + (both[R:2 * R] + cross)

        @pl.when(g // half != core)
        def _():
            exchange(g).start()

    def put(g):
        rows = rows_of(lax.rem(g, half))
        return pltpu.make_async_copy(result.at[rows], o_hbm.at[rows], out_sem.at[lax.rem(g, half)])

    def finish(g):
        @pl.when(g // half == core)
        def _():
            exchange(g).wait_recv()
            rows = rows_of(lax.rem(g, half))
            result[rows, :] = 2.0 * slab[rows, :] - (share[rows_of(g), :] + other[rows, :])
            put(g).start()

    def site(d, j):
        k, up = j // 2, j % 2
        dist = d - (k > 0).astype(jnp.int32)
        zb = z + dist - 2 * dist * up
        fine = jnp.logical_and(jnp.logical_and(zb >= 0, zb < Z), jnp.logical_and(dist >= up, dist < Z))
        return zb * X + lax.rem(x + k, X), fine, k > 0

    def work(d):
        @pl.loop(0, 2 * X)
        def _(j):
            g, fine, came_x = site(d, j)

            @pl.when(fine)
            def _():
                @pl.when(came_x)
                def _():
                    pltpu.make_async_remote_copy(
                        a_all.at[rows_of(g)], a_all.at[rows_of(g)], xsend.at[0, 0], xrecv.at[g],
                        device_id={"grid": beside(1)}, device_id_type=MESH).wait_recv()

                compute(g)

    def conclude(d):
        @pl.loop(0, 2 * X)
        def _(j):
            g, fine, _ = site(d, j)

            @pl.when(fine)
            def _():
                finish(g)

    own_load.wait()
    for part in range(b_parts):
        b_loads[part].wait()

        @pl.loop(0, b_rows // 32)
        def _(i):
            rows = pl.ds(pl.multiple_of(part * b_rows + i * 32, 32), 32)
            high, low = split(b_raw[rows, :])
            b_high[rows, :] = high
            b_low[rows, :] = low

    slab_load.wait()
    compute(grid_at)

    @pl.loop(1, Z)
    def _(d):
        for c in range(C):
            relay(d, c, 1)
            relay(d, c, -1)
        work(d)

        @pl.when(d == 1)
        def _():
            finish(grid_at)

        @pl.when(d > 1)
        def _():
            conclude(d - 1)

    @pl.loop(0, Z)
    def _(zb):
        block = a_all.at[rows_of(zb * X + x)]

        def sent(sem, peer):
            pltpu.make_async_remote_copy(
                block, block, sem, xrecv.at[0], device_id={"grid": peer}, device_id_type=MESH).wait_send()

        @pl.when(jnp.logical_and(zb <= z, z < Z - 1))
        def _():
            sent(zsend.at[0, zb], grid_at + X)

        @pl.when(jnp.logical_and(zb >= z, z > 0))
        def _():
            sent(zsend.at[1, zb], grid_at - X)

    work(Z)
    conclude(Z - 1)
    conclude(Z)

    @pl.loop(0, Z)
    def _(zb):
        block = a_all.at[rows_of(zb * X + x)]
        for k in range(1, X):
            pltpu.make_async_remote_copy(
                block, block, xsend.at[k - 1, zb], xrecv.at[0],
                device_id={"grid": beside(k)}, device_id_type=MESH).wait_send()

    @pl.loop(0, half)
    def _(h):
        exchange((1 - core) * half + h).wait_send()
        put(core * half + h).wait()


def lines(grid):
    short = max(s for s in range(1, grid + 1) if grid % s == 0 and s * s * s <= grid)
    return grid // short, short


def local(Z, X, row_block, column_block, density_slab):
    (R, K), N = row_block.shape, column_block.shape[1]
    G, ROWS = Z * X, Z * X * R
    C = 4 if R % 32 == 0 else 1
    b_parts = 4
    dma = pltpu.SemaphoreType.DMA
    any_space = pl.BlockSpec(memory_space=pl.ANY)
    return pl.pallas_call(
        functools.partial(kernel, Z, X, C),
        out_shape=jax.ShapeDtypeStruct(density_slab.shape, F32),
        in_specs=[any_space] * 3,
        out_specs=any_space,
        scratch_shapes=[
            pltpu.VMEM((ROWS, K), F32),
            pltpu.VMEM((K, N), F32),
            pltpu.VMEM((K, N), BF16),
            pltpu.VMEM((K, N), BF16),
            pltpu.VMEM((2 * R, K), BF16),
            pltpu.VMEM((ROWS, N), F32),
            pltpu.VMEM((ROWS // 2, N), F32),
            pltpu.VMEM((ROWS // 2, N), F32),
            pltpu.VMEM((ROWS // 2, N), F32),
            dma((2,)),
            dma((b_parts,)),
            dma((G // 2,)),
            dma((Z, C)),
            dma((G,)),
            dma((2, Z)),
            dma((max(X - 1, 1), Z)),
            dma((G // 2,)),
            dma((G // 2,)),
        ],
        compiler_params=pltpu.CompilerParams(
            collective_id=0, has_side_effects=True, vmem_limit_bytes=48 * 2**20
        ),
        cost_estimate=pl.CostEstimate(
            flops=6 * ROWS * K * N, bytes_accessed=4 * (R * K + K * N + ROWS * N), transcendentals=0
        ),
    )(row_block, column_block, density_slab)


def solution(mesh):
    Z, X = lines(mesh.shape["grid"])
    placed = (
        P(("pose", "grid"), "depth"),
        P(("pose", "depth"), "grid"),
        P(("pose", "depth"), "grid"),
    )
    return jax.shard_map(
        functools.partial(local, Z, X), mesh=mesh, in_specs=placed, out_specs=P(("pose", "depth"), "grid"),
        check_vma=False,
    )
```

```python
import functools

import jax
import jax.numpy as jnp
from jax import lax
from jax.experimental import pallas as pl
from jax.experimental.pallas import tpu as pltpu
from jax.sharding import PartitionSpec as P

MESH = pl.DeviceIdType.MESH
F32, BF16 = jnp.float32, jnp.bfloat16
TILE = 256


def split(value):
    high = value.astype(BF16)
    return high, (value - high.astype(F32)).astype(BF16)


def kernel(
    Z, X, far, pieces,
    a_hbm, b_hbm, d_hbm, result,
    a_all, b_raw, b_high, b_low, a_pair, share, other, slab,
    load_sem, b_sem, zrecv, xrecv, zsend, xsend, crecv, csend, far_recv, far_send,
):
    grid_at, core = lax.axis_index("grid"), lax.axis_index("depth")
    z, x = grid_at // X, grid_at % X
    G = Z * X
    half = G // 2
    R, K = a_hbm.shape
    N = b_hbm.shape[1]
    C = len(pieces)
    b_parts = b_sem.shape[0]
    b_rows = K // b_parts

    def rows_of(g):
        return pl.ds(pl.multiple_of(g * R, R), R)

    own_load = pltpu.make_async_copy(a_hbm, a_all.at[rows_of(grid_at)], load_sem.at[0])
    slab_load = pltpu.make_async_copy(d_hbm, slab, load_sem.at[1])
    own_load.start()
    b_loads = []
    for part in range(b_parts):
        rows = pl.ds(part * b_rows, b_rows)
        b_loads.append(pltpu.make_async_copy(b_hbm.at[rows], b_raw.at[rows], b_sem.at[part]))
        b_loads[-1].start()
    slab_load.start()

    barrier = pltpu.get_barrier_semaphore()

    @pl.when(z > 0)
    def _():
        pl.semaphore_signal(barrier, inc=1, device_id={"grid": grid_at - X}, device_id_type=MESH)

    @pl.when(z < Z - 1)
    def _():
        pl.semaphore_signal(barrier, inc=1, device_id={"grid": grid_at + X}, device_id_type=MESH)

    def beside(k):
        return z * X + lax.rem(x + k, X)

    for k in range(1, X):
        pl.semaphore_signal(barrier, inc=1, device_id={"grid": beside(k)}, device_id_type=MESH)
    pl.semaphore_signal(barrier, inc=1, device_id={"depth": 1 - core}, device_id_type=MESH)
    pl.semaphore_wait(barrier, X + (z > 0).astype(jnp.int32) + (z < Z - 1).astype(jnp.int32))

    def span(g, low, size):
        return pl.ds(pl.multiple_of(g * R + low, 8), size)

    def along_z(src, zb, c, step):
        way = 0 if step > 0 else 1
        k = max(c - C, 0)
        low, size = pieces[c] if c < C else (0, far)
        rows = span(zb * X + lax.rem(x + k, X), low, size)
        return pltpu.make_async_remote_copy(
            a_all.at[rows] if src is None else src, a_all.at[rows], zsend.at[way, zb], zrecv.at[zb, c],
            device_id={"grid": grid_at + step * X}, device_id_type=MESH)

    def along_x(src, zb, c, k):
        rows = span(zb * X + x, *pieces[c])
        return pltpu.make_async_remote_copy(
            a_all.at[rows] if src is None else src, a_all.at[rows], xsend.at[k - 1, zb], xrecv.at[zb * X + x, c],
            device_id={"grid": beside(k)}, device_id_type=MESH)

    def far_x(k):
        return pltpu.make_async_remote_copy(
            a_hbm.at[pl.ds(0, far)], a_all.at[span(grid_at, 0, far)], far_send.at[k - 1], far_recv.at[k - 1],
            device_id={"grid": beside(k)}, device_id_type=MESH)

    def both_ways(src, c):
        @pl.when(z < Z - 1)
        def _():
            along_z(src, z, c, 1).start()

        @pl.when(z > 0)
        def _():
            along_z(src, z, c, -1).start()

    if far:
        for k in range(1, X):
            far_x(k).start()
    for c in range(C):
        src = a_hbm.at[pl.ds(*pieces[c])]
        both_ways(src, c)
        for k in range(1, X):
            along_x(src, z, c, k).start()
    if far:
        both_ways(a_hbm.at[pl.ds(0, far)], C)

    def relay(d, c, step):
        zb = z - step * d

        @pl.when(jnp.logical_and(zb >= 0, zb < Z))
        def _():
            along_z(None, zb, c, step).wait_recv()
            onward = z + step

            @pl.when(jnp.logical_and(onward >= 0, onward < Z))
            def _():
                along_z(None, zb, c, step).start()

            if c < C:
                for k in range(1, X):
                    along_x(None, zb, c, k).start()

    def exchange(g, u=0, low=0, size=None):
        size = R if size is None else size
        h = lax.rem(g, half)
        return pltpu.make_async_remote_copy(
            share.at[span(g, low, size)], other.at[span(h, low, size)], csend.at[h], crecv.at[h, u],
            device_id={"depth": 1 - core}, device_id_type=MESH)

    def compute(g, u=0, low=0, size=None):
        size = R if size is None else size
        rows = span(g, low, size)
        top, rest = split(a_all[rows, :])
        a_pair[0:size, :] = top
        a_pair[size:2 * size, :] = rest

        @pl.loop(0, N // TILE)
        def _(t):
            cols = pl.ds(pl.multiple_of(t * TILE, TILE), TILE)
            both = jnp.dot(a_pair[0:2 * size, :], b_high[:, cols], preferred_element_type=F32)
            cross = jnp.dot(a_pair[0:size, :], b_low[:, cols], preferred_element_type=F32)
            share[rows, cols] = both[0:size] + (both[size:2 * size] + cross)

        @pl.when(g // half != core)
        def _():
            exchange(g, u, low, size).start()

    def finish(g, u=0, low=0, size=None):
        size = R if size is None else size

        @pl.when(g // half == core)
        def _():
            exchange(g, u, low, size).wait_recv()
            rows = span(lax.rem(g, half), low, size)
            result[rows, :] = 2.0 * slab[rows, :] - (share[span(g, low, size), :] + other[rows, :])

    def site(d, j):
        k, up = j // 2, j % 2
        dist = d - (k > 0).astype(jnp.int32)
        zb = z + dist - 2 * dist * up
        fine = jnp.logical_and(jnp.logical_and(zb >= 0, zb < Z), jnp.logical_and(dist >= up, dist < Z))
        return zb * X + lax.rem(x + k, X), fine, k > 0

    def arrived(g, c):
        rows = span(g, *pieces[c])
        pltpu.make_async_remote_copy(
            a_all.at[rows], a_all.at[rows], xsend.at[0, 0], xrecv.at[g, c],
            device_id={"grid": beside(1)}, device_id_type=MESH).wait_recv()

    def work(d):
        @pl.loop(0, 2 * X)
        def _(j):
            g, fine, came_x = site(d, j)

            @pl.when(fine)
            def _():
                @pl.when(came_x)
                def _():
                    for c in range(C):
                        arrived(g, c)

                compute(g)

    def conclude(d):
        @pl.loop(0, 2 * X)
        def _(j):
            g, fine, _ = site(d, j)

            @pl.when(fine)
            def _():
                finish(g)

    own_load.wait()
    for part in range(b_parts):
        b_loads[part].wait()

        @pl.loop(0, b_rows // 32)
        def _(i):
            rows = pl.ds(pl.multiple_of(part * b_rows + i * 32, 32), 32)
            high, low = split(b_raw[rows, :])
            b_high[rows, :] = high
            b_low[rows, :] = low

    if far:
        for k in range(1, X):
            g = beside(k)
            rows = span(g, 0, far)
            pltpu.make_async_remote_copy(
                a_all.at[rows], a_all.at[rows], far_send.at[0], far_recv.at[X - k - 1],
                device_id={"grid": g}, device_id_type=MESH).wait_recv()
            both_ways(None, C + k)
    compute(grid_at)
    slab_load.wait()

    @pl.loop(1, Z)
    def _(d):
        for c in range(C + X if far else C):
            relay(d, c, 1)
            relay(d, c, -1)
        work(d)

        @pl.when(d == 1)
        def _():
            finish(grid_at)

        @pl.when(d > 1)
        def _():
            conclude(d - 1)

    @pl.loop(0, Z)
    def _(zb):
        block = a_all.at[pl.ds(0, R + (X - 1) * far)]

        def sent(sem, peer):
            pltpu.make_async_remote_copy(
                block, block, sem, xrecv.at[0], device_id={"grid": peer}, device_id_type=MESH).wait_send()

        @pl.when(jnp.logical_and(zb <= z, z < Z - 1))
        def _():
            sent(zsend.at[0, zb], grid_at + X)

        @pl.when(jnp.logical_and(zb >= z, z > 0))
        def _():
            sent(zsend.at[1, zb], grid_at - X)

    cuts = sorted({low for low, _ in pieces[1:] if low % 16 == 0 and low * 2 >= R}) [:1]
    cuts = [0] + cuts + [R]
    units = [(u, low, high - low) for u, (low, high) in enumerate(zip(cuts, cuts[1:]))]

    def last(then):
        @pl.loop(2, 2 * X)
        def _(j):
            g, fine, _ = site(Z, j)

            @pl.when(fine)
            def _():
                then(g)

    def work_last(g):
        ready = 0
        for u, low, size in units:
            while ready < C and pieces[ready][0] < low + size:
                arrived(g, ready)
                ready += 1
            compute(g, u, low, size)

    def finish_last(g):
        for unit in units:
            finish(g, *unit)

    conclude(Z - 1)
    last(work_last)

    @pl.loop(0, Z)
    def _(zb):
        block = a_all.at[pl.ds(0, R - far)]
        for k in range(1, X):
            pltpu.make_async_remote_copy(
                block, block, xsend.at[k - 1, zb], xrecv.at[0, 0],
                device_id={"grid": beside(k)}, device_id_type=MESH).wait_send()

    if far:
        for k in range(1, X):
            far_x(k).wait_send()
    last(finish_last)

    @pl.loop(0, half)
    def _(h):
        exchange((1 - core) * half + h).wait_send()


def lines(grid):
    short = max(s for s in range(1, grid + 1) if grid % s == 0 and s * s * s <= grid)
    return grid // short, short


def local(Z, X, row_block, column_block, density_slab):
    (R, K), N = row_block.shape, column_block.shape[1]
    G, ROWS = Z * X, Z * X * R
    far = R * 3 // 16 // 8 * 8
    pieces = [(0, R)]
    if far:
        body = (R // 2 - far) // 8 * 8
        pieces = [(far, body), (R // 2, R // 4), (R // 2 + R // 4, R // 4)]
    C = len(pieces)
    b_parts = 4
    dma = pltpu.SemaphoreType.DMA
    far_space = pl.BlockSpec(memory_space=pltpu.HBM)
    return pl.pallas_call(
        functools.partial(kernel, Z, X, far, pieces),
        out_shape=pltpu.VMEM(density_slab.shape, F32),
        in_specs=[far_space] * 3,
        out_specs=pl.BlockSpec(memory_space=pltpu.VMEM),
        scratch_shapes=[
            pltpu.VMEM((ROWS, K), F32),
            pltpu.VMEM((K, N), F32),
            pltpu.VMEM((K, N), BF16),
            pltpu.VMEM((K, N), BF16),
            pltpu.VMEM((2 * R, K), BF16),
            pltpu.VMEM((ROWS, N), F32),
            pltpu.VMEM((ROWS // 2, N), F32),
            pltpu.VMEM((ROWS // 2, N), F32),
            dma((2,)),
            dma((b_parts,)),
            dma((Z, C + X)),
            dma((G, C)),
            dma((2, Z)),
            dma((max(X - 1, 1), Z)),
            dma((G // 2, 2)),
            dma((G // 2,)),
            dma((max(X - 1, 1),)),
            dma((max(X - 1, 1),)),
        ],
        compiler_params=pltpu.CompilerParams(
            collective_id=0, has_side_effects=True, vmem_limit_bytes=48 * 2**20
        ),
        cost_estimate=pl.CostEstimate(
            flops=6 * ROWS * K * N, bytes_accessed=4 * (R * K + K * N + ROWS * N), transcendentals=0
        ),
    )(*(pltpu.with_memory_space_constraint(each, pltpu.HBM) for each in (row_block, column_block, density_slab)))


def solution(mesh):
    Z, X = lines(mesh.shape["grid"])
    placed = (
        P(("pose", "grid"), "depth"),
        P(("pose", "depth"), "grid"),
        P(("pose", "depth"), "grid"),
    )
    return jax.shard_map(
        functools.partial(local, Z, X), mesh=mesh, in_specs=placed, out_specs=P(("pose", "depth"), "grid"),
        check_vma=False,
    )
```

```python
import functools

import jax
import jax.numpy as jnp
from jax import lax
from jax.experimental import pallas as pl
from jax.experimental.pallas import tpu as pltpu
from jax.sharding import PartitionSpec as P

MESH = pl.DeviceIdType.MESH
F32, BF16 = jnp.float32, jnp.bfloat16
TILE = 768
PIECE = 16


def split(value):
    high = value.astype(BF16)
    return high, (value - high.astype(F32)).astype(BF16)


def kernel(
    Z, X, far, S,
    a_hbm, b_hbm, d_hbm, result,
    a_all, b_raw, b_high, b_low, a_pair, share, other, slab,
    load_sem, b_sem, zrecv, xrecv, zsend, xsend, crecv, csend, far_recv, far_send,
):
    grid_at, core = lax.axis_index("grid"), lax.axis_index("depth")
    z, x = grid_at // X, grid_at % X
    G = Z * X
    half = G // 2
    R, K = a_hbm.shape
    N = b_hbm.shape[1]
    C = (R - far) // PIECE
    Q = R // 2 // PIECE
    relayed = C + X if far else C
    b_parts = b_sem.shape[0]
    b_rows = K // b_parts

    def rows_of(g):
        return pl.ds(pl.multiple_of(g * R, R), R)

    own_load = pltpu.make_async_copy(a_hbm, a_all.at[rows_of(grid_at)], load_sem.at[0])
    slab_load = pltpu.make_async_copy(d_hbm, slab, load_sem.at[1])
    own_load.start()
    b_loads = []
    for part in range(b_parts):
        rows = pl.ds(part * b_rows, b_rows)
        b_loads.append(pltpu.make_async_copy(b_hbm.at[rows], b_raw.at[rows], b_sem.at[part]))
        b_loads[-1].start()
    slab_load.start()

    barrier = pltpu.get_barrier_semaphore()

    @pl.when(z > 0)
    def _():
        pl.semaphore_signal(barrier, inc=1, device_id={"grid": grid_at - X}, device_id_type=MESH)

    @pl.when(z < Z - 1)
    def _():
        pl.semaphore_signal(barrier, inc=1, device_id={"grid": grid_at + X}, device_id_type=MESH)

    def beside(k):
        return z * X + lax.rem(x + k, X)

    for k in range(1, X):
        pl.semaphore_signal(barrier, inc=1, device_id={"grid": beside(k)}, device_id_type=MESH)
    pl.semaphore_signal(barrier, inc=1, device_id={"depth": 1 - core}, device_id_type=MESH)
    pl.semaphore_wait(barrier, X + (z > 0).astype(jnp.int32) + (z < Z - 1).astype(jnp.int32))

    def span(g, low, size):
        return pl.ds(pl.multiple_of(g * R + low, 8), size)

    def low_of(c):
        return jnp.where(c >= C, 0, jnp.where(c < Q, R - (Q - c) * PIECE, far + (c - Q) * PIECE))

    def along_z(src, zb, c, step):
        way = 0 if step > 0 else 1
        rows = span(zb * X + lax.rem(x + jnp.maximum(c - C, 0), X), low_of(c), PIECE)
        return pltpu.make_async_remote_copy(
            a_all.at[rows] if src is None else src, a_all.at[rows], zsend.at[way, zb], zrecv.at[zb, c],
            device_id={"grid": grid_at + step * X}, device_id_type=MESH)

    def along_x(src, zb, c, k):
        rows = span(zb * X + x, low_of(c), PIECE)
        return pltpu.make_async_remote_copy(
            a_all.at[rows] if src is None else src, a_all.at[rows], xsend.at[k - 1, zb],
            xrecv.at[zb * X + x, (c < Q).astype(jnp.int32)],
            device_id={"grid": beside(k)}, device_id_type=MESH)

    def far_x(k):
        return pltpu.make_async_remote_copy(
            a_hbm.at[pl.ds(0, far)], a_all.at[span(grid_at, 0, far)], far_send.at[k - 1], far_recv.at[k - 1],
            device_id={"grid": beside(k)}, device_id_type=MESH)

    def both_ways(src, c):
        @pl.when(z < Z - 1)
        def _():
            along_z(src, z, c, 1).start()

        @pl.when(z > 0)
        def _():
            along_z(src, z, c, -1).start()

    if far:
        for k in range(1, X):
            far_x(k).start()
    @pl.loop(0, C)
    def _(c):
        src = a_hbm.at[pl.ds(pl.multiple_of(low_of(c), 8), PIECE)]
        both_ways(src, c)
        for k in range(1, X):
            along_x(src, z, c, k).start()

    if far:
        both_ways(a_hbm.at[pl.ds(0, far)], C)

    def relay(d, c, step):
        zb = z - step * d

        @pl.when(jnp.logical_and(zb >= 0, zb < Z))
        def _():
            along_z(None, zb, c, step).wait_recv()
            onward = z + step

            @pl.when(jnp.logical_and(onward >= 0, onward < Z))
            def _():
                along_z(None, zb, c, step).start()

            @pl.when(c < C)
            def _():
                for k in range(1, X):
                    along_x(None, zb, c, k).start()

    def exchange(g, u=0, low=0, size=None):
        size = R if size is None else size
        h = lax.rem(g, half)
        return pltpu.make_async_remote_copy(
            share.at[span(g, low, size)], other.at[span(h, low, size)], csend.at[h], crecv.at[h, u],
            device_id={"depth": 1 - core}, device_id_type=MESH)

    def compute(g, u=0, low=0, size=None):
        size = R if size is None else size
        rows = span(g, low, size)
        top, rest = split(a_all[rows, :])
        a_pair[0:size, :] = top
        a_pair[size:2 * size, :] = rest

        @pl.loop(0, N // TILE)
        def _(t):
            cols = pl.ds(pl.multiple_of(t * TILE, TILE), TILE)
            both = jnp.dot(a_pair[0:2 * size, :], b_high[:, cols], preferred_element_type=F32)
            cross = jnp.dot(a_pair[0:size, :], b_low[:, cols], preferred_element_type=F32)
            share[rows, cols] = both[0:size] + (both[size:2 * size] + cross)

        @pl.when(g // half != core)
        def _():
            exchange(g, u, low, size).start()

    def finish(g, u=0, low=0, size=None):
        size = R if size is None else size

        @pl.when(g // half == core)
        def _():
            exchange(g, u, low, size).wait_recv()
            rows = span(lax.rem(g, half), low, size)
            result[rows, :] = 2.0 * slab[rows, :] - (share[span(g, low, size), :] + other[rows, :])

    def arrived(g, u):
        low, high = (R - Q * PIECE, R) if u else (far, R - Q * PIECE)
        if low == high:
            return
        rows = span(g, low, high - low)
        pltpu.make_async_remote_copy(
            a_all.at[rows], a_all.at[rows], xsend.at[0, 0], xrecv.at[g, u],
            device_id={"grid": beside(1)}, device_id_type=MESH).wait_recv()

    def blocks(dist, down, first, end, then):
        zb = z + dist - 2 * dist * down
        fine = jnp.logical_and(jnp.logical_and(zb >= 0, zb < Z), jnp.logical_and(dist >= down, dist < Z))

        @pl.loop(first, jnp.where(fine, end, first))
        def _(k):
            then(zb * X + lax.rem(x + k, X), k)

    def full(g, k):
        @pl.when(k > 0)
        def _():
            arrived(g, 1)
            arrived(g, 0)

        compute(g)

    own_load.wait()
    for part in range(b_parts):
        b_loads[part].wait()

        @pl.loop(0, b_rows // 32)
        def _(i):
            rows = pl.ds(pl.multiple_of(part * b_rows + i * 32, 32), 32)
            high, low = split(b_raw[rows, :])
            b_high[rows, :] = high
            b_low[rows, :] = low

    if far:
        for k in range(1, X):
            g = beside(k)
            rows = span(g, 0, far)
            pltpu.make_async_remote_copy(
                a_all.at[rows], a_all.at[rows], far_send.at[0], far_recv.at[X - k - 1],
                device_id={"grid": g}, device_id_type=MESH).wait_recv()
            both_ways(None, C + k)
    slab_load.wait()

    @pl.loop(0, (Z - 1) * S + 5)
    def _(s):
        d, c = s // S + 1, s % S

        @pl.when(jnp.logical_and(d < Z, c < relayed))
        def _():
            relay(d, c, 1)
            relay(d, c, -1)

        own = jnp.logical_or(c == 1, c == 2)
        beyond = jnp.logical_or(c == 7, c == 8)
        first = jnp.where(beyond, 1, 0)
        end = jnp.where(beyond, X, jnp.where(own, 1, 0))
        blocks(d - 1, jnp.where(beyond, c - 7, jnp.where(own, c - 1, 0)), first, end, full)

        old = jnp.logical_or(c == 3, c == 4)
        new = jnp.logical_or(c == 5, c == 6)
        first = jnp.where(old, 1, 0)
        end = jnp.where(old, X, jnp.where(new, 1, 0))

        @pl.when(jnp.logical_or(jnp.logical_and(old, d > 1), new))
        def _():
            blocks(
                jnp.where(old, d - 2, d - 1), jnp.where(old, c - 3, c - 5), first, end,
                lambda g, k: finish(g))

    parts = R // 2 // PIECE * PIECE * 2 == R and far > 0

    def work_half(u):
        def then(g, k):
            arrived(g, u)
            if parts:
                compute(g, u, u * (R // 2), R // 2)
            elif not u:
                compute(g)

        @pl.loop(0, 2)
        def _(down):
            blocks(Z - 1, down, 1, X, then)

    def finish_half(u):
        def then(g, k):
            if parts:
                finish(g, u, u * (R // 2), R // 2)
            elif not u:
                finish(g)

        @pl.loop(0, 2)
        def _(down):
            blocks(Z - 1, down, 1, X, then)

    work_half(1)

    @pl.loop(0, 2)
    def _(down):
        blocks(Z - 1, down, 0, 1, lambda g, k: finish(g))

    work_half(0)
    finish_half(1)

    @pl.loop(0, Z)
    def _(zb):
        block = a_all.at[pl.ds(0, R + (X - 1) * far)]
        thin = a_all.at[pl.ds(0, R - far)]

        def sent(block, sem, peer):
            pltpu.make_async_remote_copy(
                block, block, sem, xrecv.at[0, 0], device_id={"grid": peer}, device_id_type=MESH).wait_send()

        @pl.when(jnp.logical_and(zb <= z, z < Z - 1))
        def _():
            sent(block, zsend.at[0, zb], grid_at + X)

        @pl.when(jnp.logical_and(zb >= z, z > 0))
        def _():
            sent(block, zsend.at[1, zb], grid_at - X)

        for k in range(1, X):
            sent(thin, xsend.at[k - 1, zb], beside(k))

    if far:
        for k in range(1, X):
            far_x(k).wait_send()

    @pl.loop(0, half)
    def _(h):
        exchange((1 - core) * half + h).wait_send()

    finish_half(0)


def lines(grid):
    short = max(s for s in range(1, grid + 1) if grid % s == 0 and s * s * s <= grid)
    return grid // short, short


def local(Z, X, row_block, column_block, density_slab):
    (R, K), N = row_block.shape, column_block.shape[1]
    G, ROWS = Z * X, Z * X * R
    far = PIECE if R // PIECE >= 8 else 0
    C = (R - far) // PIECE
    S = max(C + X if far else C, 9)
    b_parts = 4
    dma = pltpu.SemaphoreType.DMA
    far_space = pl.BlockSpec(memory_space=pltpu.HBM)
    return pl.pallas_call(
        functools.partial(kernel, Z, X, far, S),
        out_shape=pltpu.VMEM(density_slab.shape, F32),
        in_specs=[far_space] * 3,
        out_specs=pl.BlockSpec(memory_space=pltpu.VMEM),
        scratch_shapes=[
            pltpu.VMEM((ROWS, K), F32),
            pltpu.VMEM((K, N), F32),
            pltpu.VMEM((K, N), BF16),
            pltpu.VMEM((K, N), BF16),
            pltpu.VMEM((2 * R, K), BF16),
            pltpu.VMEM((ROWS, N), F32),
            pltpu.VMEM((ROWS // 2, N), F32),
            pltpu.VMEM((ROWS // 2, N), F32),
            dma((2,)),
            dma((b_parts,)),
            dma((Z, S)),
            dma((G, 2)),
            dma((2, Z)),
            dma((max(X - 1, 1), Z)),
            dma((G // 2, 2)),
            dma((G // 2,)),
            dma((max(X - 1, 1),)),
            dma((max(X - 1, 1),)),
        ],
        compiler_params=pltpu.CompilerParams(
            collective_id=0, has_side_effects=True, vmem_limit_bytes=48 * 2**20
        ),
        cost_estimate=pl.CostEstimate(
            flops=6 * ROWS * K * N, bytes_accessed=4 * (R * K + K * N + ROWS * N), transcendentals=0
        ),
    )(*(pltpu.with_memory_space_constraint(each, pltpu.HBM) for each in (row_block, column_block, density_slab)))


def solution(mesh):
    Z, X = lines(mesh.shape["grid"])
    placed = (
        P(("pose", "grid"), "depth"),
        P(("pose", "depth"), "grid"),
        P(("pose", "depth"), "grid"),
    )
    return jax.shard_map(
        functools.partial(local, Z, X), mesh=mesh, in_specs=placed, out_specs=P(("pose", "depth"), "grid"),
        check_vma=False,
    )
```

```python
import functools

import jax
import jax.numpy as jnp
from jax import lax
from jax.experimental import pallas as pl
from jax.experimental.pallas import tpu as pltpu
from jax.sharding import PartitionSpec as P

MESH = pl.DeviceIdType.MESH
F32, BF16 = jnp.float32, jnp.bfloat16
TILE = 768
PIECE = 16


def split(value):
    high = value.astype(BF16)
    return high, (value - high.astype(F32)).astype(BF16)


def kernel(
    Z, X, far, S,
    a_hbm, b_hbm, d_hbm, result,
    a_all, b_raw, b_high, b_low, a_pair, share, other, slab,
    load_sem, b_sem, zrecv, xrecv, zsend, xsend, crecv, csend, far_recv, far_send,
):
    grid_at, core = lax.axis_index("grid"), lax.axis_index("depth")
    z, x = grid_at // X, grid_at % X
    G = Z * X
    half = G // 2
    R, K = a_hbm.shape
    N = b_hbm.shape[1]
    C = (R - far) // PIECE
    Q = R // 2 // PIECE
    relayed = C + X if far else C
    b_parts = b_sem.shape[0]
    b_rows = K // b_parts

    def rows_of(g):
        return pl.ds(pl.multiple_of(g * R, R), R)

    own_load = pltpu.make_async_copy(a_hbm, a_all.at[rows_of(grid_at)], load_sem.at[0])
    slab_load = pltpu.make_async_copy(d_hbm, slab, load_sem.at[1])
    own_load.start()
    b_loads = []
    for part in range(b_parts):
        rows = pl.ds(part * b_rows, b_rows)
        b_loads.append(pltpu.make_async_copy(b_hbm.at[rows], b_raw.at[rows], b_sem.at[part]))
        b_loads[-1].start()
    slab_load.start()

    barrier = pltpu.get_barrier_semaphore()

    @pl.when(z > 0)
    def _():
        pl.semaphore_signal(barrier, inc=1, device_id={"grid": grid_at - X}, device_id_type=MESH)

    @pl.when(z < Z - 1)
    def _():
        pl.semaphore_signal(barrier, inc=1, device_id={"grid": grid_at + X}, device_id_type=MESH)

    def beside(k):
        return z * X + lax.rem(x + k, X)

    for k in range(1, X):
        pl.semaphore_signal(barrier, inc=1, device_id={"grid": beside(k)}, device_id_type=MESH)
    pl.semaphore_signal(barrier, inc=1, device_id={"depth": 1 - core}, device_id_type=MESH)
    pl.semaphore_wait(barrier, X + (z > 0).astype(jnp.int32) + (z < Z - 1).astype(jnp.int32))

    def span(g, low, size):
        return pl.ds(pl.multiple_of(g * R + low, 8), size)

    def low_of(c):
        return jnp.where(c >= C, 0, jnp.where(c < Q, R - (Q - c) * PIECE, far + (c - Q) * PIECE))

    def along_z(src, zb, c, step):
        way = 0 if step > 0 else 1
        rows = span(zb * X + lax.rem(x + jnp.maximum(c - C, 0), X), low_of(c), PIECE)
        return pltpu.make_async_remote_copy(
            a_all.at[rows] if src is None else src, a_all.at[rows], zsend.at[way, zb], zrecv.at[zb, c],
            device_id={"grid": grid_at + step * X}, device_id_type=MESH)

    def along_x(src, zb, c, k):
        rows = span(zb * X + x, low_of(c), PIECE)
        return pltpu.make_async_remote_copy(
            a_all.at[rows] if src is None else src, a_all.at[rows], xsend.at[k - 1, zb],
            xrecv.at[zb * X + x, (c < Q).astype(jnp.int32)],
            device_id={"grid": beside(k)}, device_id_type=MESH)

    def far_x(k):
        return pltpu.make_async_remote_copy(
            a_hbm.at[pl.ds(0, far)], a_all.at[span(grid_at, 0, far)], far_send.at[k - 1], far_recv.at[k - 1],
            device_id={"grid": beside(k)}, device_id_type=MESH)

    def both_ways(src, c):
        @pl.when(z < Z - 1)
        def _():
            along_z(src, z, c, 1).start()

        @pl.when(z > 0)
        def _():
            along_z(src, z, c, -1).start()

    if far:
        for k in range(1, X):
            far_x(k).start()
    @pl.loop(0, C)
    def _(c):
        src = a_hbm.at[pl.ds(pl.multiple_of(low_of(c), 8), PIECE)]
        both_ways(src, c)
        for k in range(1, X):
            along_x(src, z, c, k).start()

    if far:
        both_ways(a_hbm.at[pl.ds(0, far)], C)

    def relay(d, c, step):
        zb = z - step * d

        @pl.when(jnp.logical_and(zb >= 0, zb < Z))
        def _():
            along_z(None, zb, c, step).wait_recv()
            onward = z + step

            @pl.when(jnp.logical_and(onward >= 0, onward < Z))
            def _():
                along_z(None, zb, c, step).start()

            @pl.when(c < C)
            def _():
                for k in range(1, X):
                    along_x(None, zb, c, k).start()

    def tile(t):
        return pl.ds(pl.multiple_of(t * TILE, TILE), TILE)

    def exchange(g, u=0, low=0, size=R, cols=pl.ds(0, N)):
        h = lax.rem(g, half)
        return pltpu.make_async_remote_copy(
            share.at[span(g, low, size), cols], other.at[span(h, low, size), cols], csend.at[h], crecv.at[h, u],
            device_id={"depth": 1 - core}, device_id_type=MESH)

    def compute(g, u=0, low=0, size=R):
        rows = span(g, low, size)
        top, rest = split(a_all[rows, :])
        a_pair[0:size, :] = top
        a_pair[size:2 * size, :] = rest

        @pl.loop(0, N // TILE)
        def _(t):
            cols = tile(t)
            both = jnp.dot(a_pair[0:2 * size, :], b_high[:, cols], preferred_element_type=F32)
            cross = jnp.dot(a_pair[0:size, :], b_low[:, cols], preferred_element_type=F32)
            share[rows, cols] = both[0:size] + (both[size:2 * size] + cross)
            if size < R:
                @pl.when(g // half != core)
                def _():
                    exchange(g, u * (N // TILE) + t, low, size, cols).start()

        if size == R:
            @pl.when(g // half != core)
            def _():
                exchange(g).start()

    def finish(g, u=0, low=0, size=R):
        rows = span(lax.rem(g, half), low, size)

        def subtract(cols):
            result[rows, cols] = 2.0 * slab[rows, cols] - (share[span(g, low, size), cols] + other[rows, cols])

        @pl.when(g // half == core)
        def _():
            if size < R:
                @pl.loop(0, N // TILE)
                def _(t):
                    exchange(g, u * (N // TILE) + t, low, size, tile(t)).wait_recv()
                    subtract(tile(t))
            else:
                exchange(g).wait_recv()
                subtract(slice(None))

    def arrived(g, u):
        low, high = (R - Q * PIECE, R) if u else (far, R - Q * PIECE)
        if low == high:
            return
        rows = span(g, low, high - low)
        pltpu.make_async_remote_copy(
            a_all.at[rows], a_all.at[rows], xsend.at[0, 0], xrecv.at[g, u],
            device_id={"grid": beside(1)}, device_id_type=MESH).wait_recv()

    def blocks(dist, down, first, end, then):
        zb = z + dist - 2 * dist * down
        fine = jnp.logical_and(jnp.logical_and(zb >= 0, zb < Z), jnp.logical_and(dist >= down, dist < Z))

        @pl.loop(first, jnp.where(fine, end, first))
        def _(k):
            then(zb * X + lax.rem(x + k, X), k)

    def full(g, k):
        @pl.when(k > 0)
        def _():
            arrived(g, 1)
            arrived(g, 0)

        compute(g)

    own_load.wait()
    for part in range(b_parts):
        b_loads[part].wait()

        @pl.loop(0, b_rows // 32)
        def _(i):
            rows = pl.ds(pl.multiple_of(part * b_rows + i * 32, 32), 32)
            high, low = split(b_raw[rows, :])
            b_high[rows, :] = high
            b_low[rows, :] = low

    if far:
        for k in range(1, X):
            g = beside(k)
            rows = span(g, 0, far)
            pltpu.make_async_remote_copy(
                a_all.at[rows], a_all.at[rows], far_send.at[0], far_recv.at[X - k - 1],
                device_id={"grid": g}, device_id_type=MESH).wait_recv()
            both_ways(None, C + k)
    slab_load.wait()

    reach = jnp.maximum(z, Z - 1 - z)

    @pl.loop(0, reach * S + 5)
    def _(s):
        d, c = s // S + 1, s % S

        @pl.when(jnp.logical_and(d <= reach, c < relayed))
        def _():
            relay(d, c, 1)
            relay(d, c, -1)

        own = jnp.logical_or(c == 1, c == 2)
        beyond = jnp.logical_or(c == 7, c == 8)
        first = jnp.where(beyond, 1, 0)
        end = jnp.where(beyond, X, jnp.where(own, 1, 0))
        blocks(d - 1, jnp.where(beyond, c - 7, jnp.where(own, c - 1, 0)), first, end, full)

        old = jnp.logical_or(c == 3, c == 4)
        new = jnp.logical_or(c == 5, c == 6)
        first = jnp.where(old, 1, 0)
        end = jnp.where(old, X, jnp.where(new, 1, 0))

        @pl.when(jnp.logical_or(jnp.logical_and(old, d > 1), new))
        def _():
            blocks(
                jnp.where(old, d - 2, d - 1), jnp.where(old, c - 3, c - 5), first, end,
                lambda g, k: finish(g))

    parts = R // 2 // PIECE * PIECE * 2 == R and far > 0

    def work_half(u):
        def then(g, k):
            arrived(g, u)
            if parts:
                compute(g, u, u * (R // 2), R // 2)
            elif not u:
                compute(g)

        @pl.loop(0, 2)
        def _(down):
            blocks(reach, down, 1, X, then)

    def finish_half(u):
        def then(g, k):
            if parts:
                finish(g, u, u * (R // 2), R // 2)
            elif not u:
                finish(g)

        @pl.loop(0, 2)
        def _(down):
            blocks(reach, down, 1, X, then)

    work_half(1)

    @pl.loop(0, 2)
    def _(down):
        blocks(reach, down, 0, 1, lambda g, k: finish(g))

    work_half(0)
    finish_half(1)

    @pl.loop(0, Z)
    def _(zb):
        block = a_all.at[pl.ds(0, R + (X - 1) * far)]
        thin = a_all.at[pl.ds(0, R - far)]

        def sent(block, sem, peer):
            pltpu.make_async_remote_copy(
                block, block, sem, xrecv.at[0, 0], device_id={"grid": peer}, device_id_type=MESH).wait_send()

        @pl.when(jnp.logical_and(zb <= z, z < Z - 1))
        def _():
            sent(block, zsend.at[0, zb], grid_at + X)

        @pl.when(jnp.logical_and(zb >= z, z > 0))
        def _():
            sent(block, zsend.at[1, zb], grid_at - X)

        for k in range(1, X):
            sent(thin, xsend.at[k - 1, zb], beside(k))

    if far:
        for k in range(1, X):
            far_x(k).wait_send()

    @pl.loop(0, half)
    def _(h):
        exchange((1 - core) * half + h).wait_send()

    finish_half(0)


def lines(grid):
    short = max(s for s in range(1, grid + 1) if grid % s == 0 and s * s * s <= grid)
    return grid // short, short


def local(Z, X, row_block, column_block, density_slab):
    (R, K), N = row_block.shape, column_block.shape[1]
    G, ROWS = Z * X, Z * X * R
    far = PIECE if R // PIECE >= 8 else 0
    C = (R - far) // PIECE
    S = max(C + X if far else C, 9)
    b_parts = 4
    dma = pltpu.SemaphoreType.DMA
    far_space = pl.BlockSpec(memory_space=pltpu.HBM)
    return pl.pallas_call(
        functools.partial(kernel, Z, X, far, S),
        out_shape=pltpu.VMEM(density_slab.shape, F32),
        in_specs=[far_space] * 3,
        out_specs=pl.BlockSpec(memory_space=pltpu.VMEM),
        scratch_shapes=[
            pltpu.VMEM((ROWS, K), F32),
            pltpu.VMEM((K, N), F32),
            pltpu.VMEM((K, N), BF16),
            pltpu.VMEM((K, N), BF16),
            pltpu.VMEM((2 * R, K), BF16),
            pltpu.VMEM((ROWS, N), F32),
            pltpu.VMEM((ROWS // 2, N), F32),
            pltpu.VMEM((ROWS // 2, N), F32),
            dma((2,)),
            dma((b_parts,)),
            dma((Z, S)),
            dma((G, 2)),
            dma((2, Z)),
            dma((max(X - 1, 1), Z)),
            dma((G // 2, 2 * N // TILE)),
            dma((G // 2,)),
            dma((max(X - 1, 1),)),
            dma((max(X - 1, 1),)),
        ],
        compiler_params=pltpu.CompilerParams(
            collective_id=0, has_side_effects=True, vmem_limit_bytes=48 * 2**20
        ),
        cost_estimate=pl.CostEstimate(
            flops=6 * ROWS * K * N, bytes_accessed=4 * (R * K + K * N + ROWS * N), transcendentals=0
        ),
    )(*(pltpu.with_memory_space_constraint(each, pltpu.HBM) for each in (row_block, column_block, density_slab)))


def solution(mesh):
    Z, X = lines(mesh.shape["grid"])
    placed = (
        P(("pose", "grid"), "depth"),
        P(("pose", "depth"), "grid"),
        P(("pose", "depth"), "grid"),
    )
    return jax.shard_map(
        functools.partial(local, Z, X), mesh=mesh, in_specs=placed, out_specs=P(("pose", "depth"), "grid"),
        check_vma=False,
    )
```

```python
import functools

import jax
import jax.numpy as jnp
from jax import lax
from jax.experimental import pallas as pl
from jax.experimental.pallas import tpu as pltpu
from jax.sharding import PartitionSpec as P

MESH = pl.DeviceIdType.MESH
F32, BF16 = jnp.float32, jnp.bfloat16
TILE = 1536
PIECE = 16


def split(value):
    high = value.astype(BF16)
    return high, (value - high.astype(F32)).astype(BF16)


def kernel(
    Z, X, far, S,
    a_hbm, b_hbm, d_hbm, result,
    a_all, b_raw, b_high, b_low, a_pair, share, other, slab,
    load_sem, b_sem, zrecv, xrecv, zsend, xsend, crecv, csend, far_recv, far_send,
):
    grid_at, core = lax.axis_index("grid"), lax.axis_index("depth")
    z, x = grid_at // X, grid_at % X
    G = Z * X
    half = G // 2
    R, K = a_hbm.shape
    N = b_hbm.shape[1]
    C = (R - far) // PIECE
    Q = R // 2 // PIECE
    relayed = C + X if far else C
    b_parts = b_sem.shape[0]
    b_rows = K // b_parts

    def rows_of(g):
        return pl.ds(pl.multiple_of(g * R, R), R)

    own_load = pltpu.make_async_copy(a_hbm, a_all.at[rows_of(grid_at)], load_sem.at[0])
    slab_load = pltpu.make_async_copy(d_hbm, slab, load_sem.at[1])
    own_load.start()
    b_loads = []
    for part in range(b_parts):
        rows = pl.ds(part * b_rows, b_rows)
        b_loads.append(pltpu.make_async_copy(b_hbm.at[rows], b_raw.at[rows], b_sem.at[part]))
        b_loads[-1].start()
    slab_load.start()

    barrier = pltpu.get_barrier_semaphore()

    @pl.when(z > 0)
    def _():
        pl.semaphore_signal(barrier, inc=1, device_id={"grid": grid_at - X}, device_id_type=MESH)

    @pl.when(z < Z - 1)
    def _():
        pl.semaphore_signal(barrier, inc=1, device_id={"grid": grid_at + X}, device_id_type=MESH)

    def beside(k):
        return z * X + lax.rem(x + k, X)

    for k in range(1, X):
        pl.semaphore_signal(barrier, inc=1, device_id={"grid": beside(k)}, device_id_type=MESH)
    pl.semaphore_signal(barrier, inc=1, device_id={"depth": 1 - core}, device_id_type=MESH)
    pl.semaphore_wait(barrier, X + (z > 0).astype(jnp.int32) + (z < Z - 1).astype(jnp.int32))

    def span(g, low, size):
        return pl.ds(pl.multiple_of(g * R + low, 8), size)

    def low_of(c):
        return jnp.where(c >= C, 0, jnp.where(c < Q, R - (Q - c) * PIECE, far + (c - Q) * PIECE))

    def along_z(src, zb, c, step):
        way = 0 if step > 0 else 1
        rows = span(zb * X + lax.rem(x + jnp.maximum(c - C, 0), X), low_of(c), PIECE)
        return pltpu.make_async_remote_copy(
            a_all.at[rows] if src is None else src, a_all.at[rows], zsend.at[way, zb], zrecv.at[zb, c],
            device_id={"grid": grid_at + step * X}, device_id_type=MESH)

    def along_x(src, zb, c, k):
        rows = span(zb * X + x, low_of(c), PIECE)
        return pltpu.make_async_remote_copy(
            a_all.at[rows] if src is None else src, a_all.at[rows], xsend.at[k - 1, zb],
            xrecv.at[zb * X + x, (c < Q).astype(jnp.int32)],
            device_id={"grid": beside(k)}, device_id_type=MESH)

    def far_x(k):
        return pltpu.make_async_remote_copy(
            a_hbm.at[pl.ds(0, far)], a_all.at[span(grid_at, 0, far)], far_send.at[k - 1], far_recv.at[k - 1],
            device_id={"grid": beside(k)}, device_id_type=MESH)

    def both_ways(src, c):
        @pl.when(z < Z - 1)
        def _():
            along_z(src, z, c, 1).start()

        @pl.when(z > 0)
        def _():
            along_z(src, z, c, -1).start()

    if far:
        for k in range(1, X):
            far_x(k).start()
    @pl.loop(0, C)
    def _(c):
        src = a_hbm.at[pl.ds(pl.multiple_of(low_of(c), 8), PIECE)]
        both_ways(src, c)
        for k in range(1, X):
            along_x(src, z, c, k).start()

    if far:
        both_ways(a_hbm.at[pl.ds(0, far)], C)

    def relay(d, c, step):
        zb = z - step * d

        @pl.when(jnp.logical_and(zb >= 0, zb < Z))
        def _():
            along_z(None, zb, c, step).wait_recv()
            onward = z + step

            @pl.when(jnp.logical_and(onward >= 0, onward < Z))
            def _():
                along_z(None, zb, c, step).start()

            @pl.when(c < C)
            def _():
                for k in range(1, X):
                    along_x(None, zb, c, k).start()

    def tile(t):
        return pl.ds(pl.multiple_of(t * TILE, TILE), TILE)

    def exchange(g, u=0, low=0, size=R, cols=pl.ds(0, N)):
        h = lax.rem(g, half)
        return pltpu.make_async_remote_copy(
            share.at[span(g, low, size), cols], other.at[span(h, low, size), cols], csend.at[h], crecv.at[h, u],
            device_id={"depth": 1 - core}, device_id_type=MESH)

    def compute(g, u=0, low=0, size=R):
        rows = span(g, low, size)
        top, rest = split(a_all[rows, :])
        a_pair[0:size, :] = top
        a_pair[size:2 * size, :] = rest

        @pl.loop(0, N // TILE)
        def _(t):
            cols = tile(t)
            both = jnp.dot(a_pair[0:2 * size, :], b_high[:, cols], preferred_element_type=F32)
            cross = jnp.dot(a_pair[0:size, :], b_low[:, cols], preferred_element_type=F32)
            share[rows, cols] = both[0:size] + (both[size:2 * size] + cross)
            if size < R:
                @pl.when(g // half != core)
                def _():
                    exchange(g, u * (N // TILE) + t, low, size, cols).start()

        if size == R:
            @pl.when(g // half != core)
            def _():
                exchange(g).start()

    def finish(g, u=0, low=0, size=R):
        rows = span(lax.rem(g, half), low, size)

        def subtract(cols):
            result[rows, cols] = 2.0 * slab[rows, cols] - (share[span(g, low, size), cols] + other[rows, cols])

        @pl.when(g // half == core)
        def _():
            if size < R:
                @pl.loop(0, N // TILE)
                def _(t):
                    exchange(g, u * (N // TILE) + t, low, size, tile(t)).wait_recv()
                    subtract(tile(t))
            else:
                exchange(g).wait_recv()
                subtract(slice(None))

    def arrived(g, u):
        low, high = (R - Q * PIECE, R) if u else (far, R - Q * PIECE)
        if low == high:
            return
        rows = span(g, low, high - low)
        pltpu.make_async_remote_copy(
            a_all.at[rows], a_all.at[rows], xsend.at[0, 0], xrecv.at[g, u],
            device_id={"grid": beside(1)}, device_id_type=MESH).wait_recv()

    def blocks(dist, down, first, end, then):
        zb = z + dist - 2 * dist * down
        fine = jnp.logical_and(jnp.logical_and(zb >= 0, zb < Z), jnp.logical_and(dist >= down, dist < Z))

        @pl.loop(first, jnp.where(fine, end, first))
        def _(k):
            then(zb * X + lax.rem(x + k, X), k)

    def full(g, k):
        @pl.when(k > 0)
        def _():
            arrived(g, 1)
            arrived(g, 0)

        compute(g)

    own_load.wait()
    for part in range(b_parts):
        b_loads[part].wait()

        @pl.loop(0, b_rows // 32)
        def _(i):
            rows = pl.ds(pl.multiple_of(part * b_rows + i * 32, 32), 32)
            high, low = split(b_raw[rows, :])
            b_high[rows, :] = high
            b_low[rows, :] = low

    if far:
        for k in range(1, X):
            g = beside(k)
            rows = span(g, 0, far)
            pltpu.make_async_remote_copy(
                a_all.at[rows], a_all.at[rows], far_send.at[0], far_recv.at[X - k - 1],
                device_id={"grid": g}, device_id_type=MESH).wait_recv()
            both_ways(None, C + k)
    slab_load.wait()

    reach = jnp.maximum(z, Z - 1 - z)

    @pl.loop(0, reach * S + 5)
    def _(s):
        d, c = s // S + 1, s % S

        @pl.when(jnp.logical_and(d <= reach, c < relayed))
        def _():
            relay(d, c, 1)
            relay(d, c, -1)

        own = jnp.logical_or(c == 1, c == 2)
        beyond = jnp.logical_or(c == 7, c == 8)
        first = jnp.where(beyond, 1, 0)
        end = jnp.where(beyond, X, jnp.where(own, 1, 0))
        blocks(d - 1, jnp.where(beyond, c - 7, jnp.where(own, c - 1, 0)), first, end, full)

        old = jnp.logical_or(c == 3, c == 4)
        new = jnp.logical_or(c == 5, c == 6)
        first = jnp.where(old, 1, 0)
        end = jnp.where(old, X, jnp.where(new, 1, 0))

        @pl.when(jnp.logical_or(jnp.logical_and(old, d > 1), new))
        def _():
            blocks(
                jnp.where(old, d - 2, d - 1), jnp.where(old, c - 3, c - 5), first, end,
                lambda g, k: finish(g))

    parts = R // 2 // PIECE * PIECE * 2 == R and far > 0

    def work_half(u):
        def then(g, k):
            arrived(g, u)
            if parts:
                compute(g, u, u * (R // 2), R // 2)
            elif not u:
                compute(g)

        @pl.loop(0, 2)
        def _(down):
            blocks(reach, down, 1, X, then)

    def finish_half(u):
        def then(g, k):
            if parts:
                finish(g, u, u * (R // 2), R // 2)
            elif not u:
                finish(g)

        @pl.loop(0, 2)
        def _(down):
            blocks(reach, down, 1, X, then)

    work_half(1)

    @pl.loop(0, 2)
    def _(down):
        blocks(reach, down, 0, 1, lambda g, k: finish(g))

    work_half(0)
    finish_half(1)

    @pl.loop(0, Z)
    def _(zb):
        block = a_all.at[pl.ds(0, R + (X - 1) * far)]
        thin = a_all.at[pl.ds(0, R - far)]

        def sent(block, sem, peer):
            pltpu.make_async_remote_copy(
                block, block, sem, xrecv.at[0, 0], device_id={"grid": peer}, device_id_type=MESH).wait_send()

        @pl.when(jnp.logical_and(zb <= z, z < Z - 1))
        def _():
            sent(block, zsend.at[0, zb], grid_at + X)

        @pl.when(jnp.logical_and(zb >= z, z > 0))
        def _():
            sent(block, zsend.at[1, zb], grid_at - X)

        for k in range(1, X):
            sent(thin, xsend.at[k - 1, zb], beside(k))

    if far:
        for k in range(1, X):
            far_x(k).wait_send()

    @pl.loop(0, half)
    def _(h):
        exchange((1 - core) * half + h).wait_send()

    finish_half(0)


def lines(grid):
    short = max(s for s in range(1, grid + 1) if grid % s == 0 and s * s * s <= grid)
    return grid // short, short


def local(Z, X, row_block, column_block, density_slab):
    (R, K), N = row_block.shape, column_block.shape[1]
    G, ROWS = Z * X, Z * X * R
    far = PIECE if R // PIECE >= 8 else 0
    C = (R - far) // PIECE
    S = max(C + X if far else C, 9)
    b_parts = 4
    dma = pltpu.SemaphoreType.DMA
    far_space = pl.BlockSpec(memory_space=pltpu.HBM)
    return pl.pallas_call(
        functools.partial(kernel, Z, X, far, S),
        out_shape=pltpu.VMEM(density_slab.shape, F32),
        in_specs=[far_space] * 3,
        out_specs=pl.BlockSpec(memory_space=pltpu.VMEM),
        scratch_shapes=[
            pltpu.VMEM((ROWS, K), F32),
            pltpu.VMEM((K, N), F32),
            pltpu.VMEM((K, N), BF16),
            pltpu.VMEM((K, N), BF16),
            pltpu.VMEM((2 * R, K), BF16),
            pltpu.VMEM((ROWS, N), F32),
            pltpu.VMEM((ROWS // 2, N), F32),
            pltpu.VMEM((ROWS // 2, N), F32),
            dma((2,)),
            dma((b_parts,)),
            dma((Z, S)),
            dma((G, 2)),
            dma((2, Z)),
            dma((max(X - 1, 1), Z)),
            dma((G // 2, 2 * N // TILE)),
            dma((G // 2,)),
            dma((max(X - 1, 1),)),
            dma((max(X - 1, 1),)),
        ],
        compiler_params=pltpu.CompilerParams(
            collective_id=0, has_side_effects=True, vmem_limit_bytes=48 * 2**20
        ),
        cost_estimate=pl.CostEstimate(
            flops=6 * ROWS * K * N, bytes_accessed=4 * (R * K + K * N + ROWS * N), transcendentals=0
        ),
    )(*(pltpu.with_memory_space_constraint(each, pltpu.HBM) for each in (row_block, column_block, density_slab)))


def solution(mesh):
    Z, X = lines(mesh.shape["grid"])
    placed = (
        P(("pose", "grid"), "depth"),
        P(("pose", "depth"), "grid"),
        P(("pose", "depth"), "grid"),
    )
    return jax.shard_map(
        functools.partial(local, Z, X), mesh=mesh, in_specs=placed, out_specs=P(("pose", "depth"), "grid"),
        check_vma=False,
    )
```
